32 devices in a mesh: prow: 8 (over y, x, core), pcol: 4 (over z).
Axes of the slice: x: 2, y: 2, z: 4, core: 2. Of those that a mesh axis runs over, the one named last changes fastest.
Arguments:
- inverse_block: float32 [3, 8, 256, 6, 4, 256], P(None, 'prow', None, None, 'pcol'), as said below
- panel_first: float32 [3, 8, 256, 512], P(None, 'prow', 'pcol'), may hold values from -0.078125 to 0.078125
- panel_second: float32 [3, 8, 256, 512], P(None, 'prow', 'pcol'), may hold values from -0.078125 to 0.078125
- diag_first: float32 [512, 512], replicated, may hold values from -6 to 6
- diag_second: float32 [512, 512], replicated, may hold values from -6 to 6
- pattern_first: int32 [24], replicated, may hold values from 0 to 1, as said below
- pattern_second: int32 [24], replicated, may hold values from 0 to 1, as said below
Outputs:
- column_first: float32 [3, 8, 256, 512], P(None, 'prow', 'pcol')
- column_second: float32 [3, 8, 256, 512], P(None, 'prow', 'pcol')
- diagonal_first: float32 [512, 512], replicated
- diagonal_second: float32 [512, 512], replicated
The draws below stay inside these ranges and needn't reach their ends.
Inputs may be any that keep to these rules, and one draw needn't show every extreme that they name: inverse_block is symmetric as a matrix of 6144 rows: its entry (i, j) equals its entry (j, i) exactly. `pattern_first`: at least one entry is 1. `pattern_second`: at least one entry is 1.
All inputs are finite; a program needn't handle non-finite values.
Results may differ from the reference program's by a relative error of at most 0.000071.
Values sent between devices are 32-bit elements; how exact they have to be, the bound alone decides.
A program may use at most 64 MiB of HBM per device.

```python
import jax
import jax.numpy as jnp
from jax import lax

SB = 256
W = 512
NBR_LOC = 3
PROWS = 8
PCOLS = 4
NB = 24
NBC_LOC = 6


def draw_inverse_block(key, part):
    order_rows = NB * SB
    base = jax.random.normal(key, (order_rows, order_rows), jnp.float32)
    symmetric = (base + base.T) * 0.70710678
    return symmetric.reshape(NBR_LOC, PROWS, SB, NBC_LOC, PCOLS, SB)


def pattern_bits(key):
    bits = jax.random.randint(key, (NB,), 0, 2, jnp.int32)
    place = jax.random.randint(jax.random.fold_in(key, 7), (), 0, NB, jnp.int32)
    return bits.at[place].set(1)


def draw_pattern_first(key, part):
    return pattern_bits(jax.random.fold_in(key, 101))


def draw_pattern_second(key, part):
    return pattern_bits(jax.random.fold_in(key, 202))


def level_of(stream_key, shape, split, low, largest):
    factor_of, own = 1.0, jax.random.fold_in(stream_key, 6)
    for axis_at, parts in split:
        draws = jnp.exp(jax.random.uniform(jax.random.fold_in(own, axis_at), (parts,), jnp.float32, low / len(split), largest / len(split)))
        factor_of = factor_of * jnp.repeat(draws, shape[axis_at] // parts).reshape([-1 if axis == axis_at else 1 for axis in range(len(shape))])
    return factor_of


def normal_values(stream_key, shape, width, reach, split=(), held_as=jnp.bfloat16):
    values = jax.random.normal(stream_key, shape, jnp.float32) * width
    if len(split) > 0:
        values = level_of(stream_key, shape, split, -0.22, 0.18) * values
    return jnp.clip(values, min=-reach, max=reach).astype(held_as)


def setup_inputs(seed: int = 0) -> dict:
    streams_of = jax.random.split(jax.random.key(seed), 8)
    inverse_block = draw_inverse_block(jax.random.fold_in(streams_of[7], 71), 0)
    panel_first = normal_values(streams_of[1], (NBR_LOC, PROWS, SB, W), (NB * SB) ** -0.5, 0.078125, ((1, 8), (2, 4)), jnp.float32)
    panel_second = normal_values(streams_of[2], (NBR_LOC, PROWS, SB, W), (NB * SB) ** -0.5, 0.078125, ((1, 8), (2, 4)), jnp.float32)
    diag_first = normal_values(streams_of[3], (W, W), 1.0, 6.0, (), jnp.float32)
    diag_second = normal_values(streams_of[4], (W, W), 1.0, 6.0, (), jnp.float32)
    pattern_first = draw_pattern_first(jax.random.fold_in(streams_of[7], 71), 0)
    pattern_second = draw_pattern_second(jax.random.fold_in(streams_of[7], 71), 0)
    return {"inverse_block": inverse_block, "panel_first": panel_first, "panel_second": panel_second, "diag_first": diag_first, "diag_second": diag_second, "pattern_first": pattern_first, "pattern_second": pattern_second}


def one_column(matrix, panel_part, pattern, diag_term):
    order_rows = NB * SB
    kept_mask = jnp.repeat(pattern.astype(jnp.float32), SB)[:, None]
    kept_panel = panel_part.reshape(order_rows, W) * kept_mask
    product = jnp.dot(matrix, kept_panel, precision=lax.Precision.HIGHEST, preferred_element_type=jnp.float32)
    result = -(product * kept_mask)
    diagonal = diag_term - jnp.dot(kept_panel.T, result, precision=lax.Precision.HIGHEST, preferred_element_type=jnp.float32)
    return result.reshape(NBR_LOC, PROWS, SB, W), diagonal


def reference(inverse_block, panel_first, panel_second, diag_first, diag_second, pattern_first, pattern_second):
    matrix = inverse_block.reshape(NB * SB, NB * SB)
    first_col, first_diag = one_column(matrix, panel_first, pattern_first, diag_first)
    second_col, second_diag = one_column(matrix, panel_second, pattern_second, diag_second)
    return (first_col, second_col, first_diag, second_diag)
```

```python
import functools

import jax
import jax.numpy as jnp
from jax import lax
from jax.experimental import pallas as pl
from jax.experimental.pallas import tpu as pltpu
from jax.sharding import PartitionSpec as P

MESH = pl.DeviceIdType.MESH
LANES = 128
F32 = jnp.float32
BF16 = jnp.bfloat16


def halves(value):
    high = value.astype(BF16)
    return high, (value - high.astype(F32)).astype(BF16)


def dot3(left, right, dims):
    def one(a, b):
        return lax.dot_general(a, b, (dims, ((), ())), preferred_element_type=F32)

    return one(left[0], right[0]) + (one(left[0], right[1]) + one(left[1], right[0]))


def kernel(
    sizes,
    mat,
    p0,
    p1,
    pat0,
    pat1,
    col0,
    col1,
    dia0,
    dia1,
    xbuf,
    ahi,
    alo,
    xhi,
    xlo,
    ybuf,
    rsbuf,
    khi,
    klo,
    chi,
    clo,
    dpart,
    drecv,
    dsum,
    zbuf,
    s1_send,
    s1_recv,
    ag_send,
    ag_recv,
    sib_send,
    sib_recv,
    rs_send,
    rs_recv,
    dr_send,
    dr_recv,
    dz_send,
    dz_recv,
    da_send,
    da_recv,
):
    R, C, L, B, S, W = sizes
    F = R // C
    lane_parts = W // LANES
    RC = R // lane_parts
    r = lax.axis_index("prow")
    c = lax.axis_index("pcol")
    panels, pats, cols, dias = (p0, p1), (pat0, pat1), (col0, col1), (dia0, dia1)
    total = R * C
    me = r * C + c
    sibling = r + 1 - 2 * lax.rem(r, 2)

    barrier = pltpu.get_barrier_semaphore()

    @pl.loop(1, total)
    def _(i):
        other = lax.rem(me + i, total)
        pl.semaphore_signal(
            barrier, inc=1, device_id=(lax.div(other, C), lax.rem(other, C)), device_id_type=MESH
        )

    pl.semaphore_wait(barrier, total - 1)

    def row_part(k):
        return lax.div(k, lane_parts)

    def lanes(k):
        return pl.ds(pl.multiple_of(lax.rem(k, lane_parts) * LANES, LANES), LANES)

    def remote(src, dst, send, recv, row, column):
        return pltpu.make_async_remote_copy(
            src_ref=src,
            dst_ref=dst,
            send_sem=send,
            recv_sem=recv,
            device_id=(row, column),
            device_id_type=MESH,
        )

    plane = lax.rem(r, C)
    source = lax.div(r, C) * C + c
    own_plane = plane == c

    def first_copy(n, d):
        k = lax.rem(r + d, R)
        src = panels[n].at[:, row_part(k), :, lanes(k)]
        dst = xbuf.at[n, :, source, row_part(k), :, lanes(k)]
        return remote(src, dst, s1_send.at[n, d], s1_recv.at[n, source], k, plane)

    def first_local(n):
        src = panels[n].at[:, row_part(r), :, lanes(r)]
        dst = xbuf.at[n, :, source, row_part(r), :, lanes(r)]
        return pltpu.make_async_copy(src, dst, s1_recv.at[n, source])

    def first_wait(n, q):
        part = xbuf.at[n, :, q, row_part(r), :, lanes(r)]
        pltpu.make_async_copy(part, part, s1_recv.at[n, q]).wait()

    def strip(n, k):
        return xbuf.at[n, :, :, row_part(k), :, lanes(k)]

    def gather_copy(n, j):
        part = strip(n, r)
        return remote(
            part, part, ag_send.at[n, j], ag_recv.at[n, j], lax.rem(r + 2 * j, R), c
        )

    def gather_wait(n, j):
        part = strip(n, lax.rem(r + R - 2 * j, R))
        pltpu.make_async_copy(part, part, ag_recv.at[n, j]).wait()

    def sibling_copy(n, j):
        part = strip(n, lax.rem(r + R - 2 * j, R))
        return remote(part, part, sib_send.at[n, j], sib_recv.at[n, j], sibling, c)

    def sibling_wait(n, j):
        part = strip(n, lax.rem(sibling + R - 2 * j, R))
        pltpu.make_async_copy(part, part, sib_recv.at[n, j]).wait()

    def scatter_copy(n, d):
        z = lax.rem(c + d, C)
        return remote(
            ybuf.at[n, :, pl.ds(pl.multiple_of(z * S, S), S), :],
            rsbuf.at[n, d],
            rs_send.at[n, d],
            rs_recv.at[n, d],
            r,
            z,
        )

    def diag_row_copy(n, d):
        k = lax.rem(r + d, R)
        return remote(
            dpart.at[n, k], drecv.at[n, d], dr_send.at[n, d], dr_recv.at[n, d], k, c
        )

    def diag_col_copy(n, d):
        return remote(
            dsum.at[n], zbuf.at[n, d], dz_send.at[n, d], dz_recv.at[n, d], r, lax.rem(c + d, C)
        )

    def diag_all_copy(n, d):
        return remote(
            dias[n].at[r], dias[n].at[r], da_send.at[n, d], da_recv.at[n, d], lax.rem(r + d, R), c
        )

    def diag_all_wait(n, d):
        part = dias[n].at[lax.rem(r + R - d, R)]
        pltpu.make_async_copy(part, part, da_recv.at[n, d]).wait()

    def start_first(n):
        for d in range(1, R):
            first_copy(n, d).start()

        @pl.when(own_plane)
        def _():
            first_local(n).start()

        @pl.when(jnp.logical_not(own_plane))
        def _():
            first_copy(n, 0).start()

    def start_gather(n):
        for q in range(F * C):
            first_wait(n, q)
        for j in range(1, R // 2):
            gather_copy(n, j).start()
        sibling_copy(n, 0).start()

    def forward(n):
        for j in range(1, R // 2):
            gather_wait(n, j)
            sibling_copy(n, j).start()

    def multiply(n):
        for j in range(R // 2):
            sibling_wait(n, j)

        @pl.loop(0, L * F * C)
        def _(i):
            l = lax.div(i, F * C)
            q = lax.rem(i, F * C)
            kept = pats[n][l * R + lax.div(q, C) * C + c].astype(F32)
            rows = pl.ds(pl.multiple_of(i * S, S), S)
            high, low = halves(xbuf[n, l, q].reshape(S, W) * kept)
            xhi[rows, :] = high
            xlo[rows, :] = low

        @pl.loop(0, L)
        def _(l):
            rows = pl.ds(pl.multiple_of(l * B, B), B)
            ybuf[n, l] = dot3(
                (ahi[rows, :], alo[rows, :]), (xhi[...], xlo[...]), ((1,), (0,))
            )

        for d in range(1, C):
            scatter_copy(n, d).start()

    def finish_column(n):
        for d in range(1, C):
            scatter_copy(n, d).wait_recv()
        for l in range(L):
            kept = pats[n][l * R + r].astype(F32)
            value = ybuf[n, l, pl.ds(pl.multiple_of(c * S, S), S), :]
            for d in range(1, C):
                value = value + rsbuf[n, d, l]
            value = -(value * kept)
            cols[n][l] = value
            rows = slice(l * S, (l + 1) * S)
            chi[rows, :], clo[rows, :] = halves(value)
            khi[rows, :], klo[rows, :] = halves(panels[n][l].reshape(S, W) * kept)
        part = dot3((khi[...], klo[...]), (chi[...], clo[...]), ((0,), (0,)))
        dpart[n] = part.reshape(R, W // R, W)
        for d in range(1, R):
            diag_row_copy(n, d).start()

    def diag_rows(n):
        value = dpart[n, r]
        for d in range(1, R):
            diag_row_copy(n, d).wait_recv()
            value = value + drecv[n, d]
        dsum[n] = value
        for d in range(1, C):
            diag_col_copy(n, d).start()

    def diag_cols(n):
        value = dsum[n]
        for d in range(1, C):
            diag_col_copy(n, d).wait_recv()
            value = value + zbuf[n, d]
        dias[n][r] = value
        for d in range(1, R):
            diag_all_copy(n, d).start()

    start_first(0)
    start_first(1)

    tile = min(B, 64)

    @pl.loop(0, L * B // tile)
    def _(i):
        rows = pl.ds(pl.multiple_of(i * tile, tile), tile)
        ahi[rows, :], alo[rows, :] = halves(mat[rows, :])

    start_gather(0)
    forward(0)
    start_gather(1)
    multiply(0)
    forward(1)
    multiply(1)
    finish_column(0)
    diag_rows(0)
    finish_column(1)
    diag_cols(0)
    diag_rows(1)
    diag_cols(1)
    for n in range(2):
        for d in range(1, R):
            diag_all_wait(n, d)
        for d in range(1, R):
            first_copy(n, d).wait_send()
            diag_row_copy(n, d).wait_send()
            diag_all_copy(n, d).wait_send()

        @pl.when(jnp.logical_not(own_plane))
        def _():
            first_copy(n, 0).wait_send()

        for j in range(R // 2):
            if j > 0:
                gather_copy(n, j).wait_send()
            sibling_copy(n, j).wait_send()
        for d in range(1, C):
            scatter_copy(n, d).wait_send()
            diag_col_copy(n, d).wait_send()


def body(R, C, inverse, first, second, diag_first, diag_second, pat_first, pat_second):
    L, _, B, M, _, _ = inverse.shape
    S, W = first.shape[2:]
    F = R // C
    RC = R // (W // LANES)
    matrix = inverse.reshape(L * B, M * B)
    panels = [p.reshape(L, RC, S // RC, W) for p in (first, second)]
    vmem = pl.BlockSpec(memory_space=pltpu.VMEM)
    smem = pl.BlockSpec(memory_space=pltpu.SMEM)
    dma = pltpu.SemaphoreType.DMA
    part = W // R
    flops = 3 * 2 * L * B * M * B * 2 * W
    col0, col1, sum0, sum1 = pl.pallas_call(
        functools.partial(kernel, (R, C, L, B, S, W)),
        out_shape=[jax.ShapeDtypeStruct((L, S, W), F32)] * 2
        + [jax.ShapeDtypeStruct((R, part, W), F32)] * 2,
        in_specs=[vmem] * 3 + [smem] * 2,
        out_specs=[vmem] * 4,
        scratch_shapes=[
            pltpu.VMEM((2, L, F * C, RC, S // RC, W), F32),
            pltpu.VMEM((L * B, M * B), BF16),
            pltpu.VMEM((L * B, M * B), BF16),
            pltpu.VMEM((M * B, W), BF16),
            pltpu.VMEM((M * B, W), BF16),
            pltpu.VMEM((2, L, B, W), F32),
            pltpu.VMEM((2, C, L, S, W), F32),
            pltpu.VMEM((L * S, W), BF16),
            pltpu.VMEM((L * S, W), BF16),
            pltpu.VMEM((L * S, W), BF16),
            pltpu.VMEM((L * S, W), BF16),
            pltpu.VMEM((2, R, part, W), F32),
            pltpu.VMEM((2, R, part, W), F32),
            pltpu.VMEM((2, part, W), F32),
            pltpu.VMEM((2, C, part, W), F32),
            dma((2, R)),
            dma((2, F * C)),
            dma((2, R // 2)),
            dma((2, R // 2)),
            dma((2, R // 2)),
            dma((2, R // 2)),
            dma((2, C)),
            dma((2, C)),
            dma((2, R)),
            dma((2, R)),
            dma((2, C)),
            dma((2, C)),
            dma((2, R)),
            dma((2, R)),
        ],
        compiler_params=pltpu.CompilerParams(
            collective_id=0, has_side_effects=True, vmem_limit_bytes=56 * 1024 * 1024
        ),
        cost_estimate=pl.CostEstimate(
            flops=flops, bytes_accessed=4 * L * B * M * B, transcendentals=0
        ),
    )(matrix, *panels, pat_first, pat_second)
    return (
        col0[:, None],
        col1[:, None],
        diag_first - sum0.reshape(W, W),
        diag_second - sum1.reshape(W, W),
    )


def solution(mesh):
    placed = (
        P(None, "prow", None, None, "pcol", None),
        P(None, "prow", "pcol", None),
        P(None, "prow", "pcol", None),
        P(),
        P(),
        P(),
        P(),
    )
    return jax.shard_map(
        functools.partial(body, mesh.shape["prow"], mesh.shape["pcol"]),
        mesh=mesh,
        in_specs=placed,
        out_specs=(P(None, "prow", "pcol", None), P(None, "prow", "pcol", None), P(), P()),
        check_vma=False,
    )
```

```python
import functools

import jax
import jax.numpy as jnp
from jax import lax
from jax.experimental import pallas as pl
from jax.experimental.pallas import tpu as pltpu
from jax.sharding import PartitionSpec as P

MESH = pl.DeviceIdType.MESH
LANES = 128
F32 = jnp.float32
BF16 = jnp.bfloat16


def halves(value):
    high = value.astype(BF16)
    return high, (value - high.astype(F32)).astype(BF16)


def dot3(left, right, dims):
    def one(a, b):
        return lax.dot_general(a, b, (dims, ((), ())), preferred_element_type=F32)

    return one(left[0], right[0]) + (one(left[0], right[1]) + one(left[1], right[0]))


def kernel(
    sizes,
    mat,
    p0,
    p1,
    pat0,
    pat1,
    col0,
    col1,
    dia0,
    dia1,
    xbuf,
    ahi,
    alo,
    xhi,
    xlo,
    ybuf,
    downbuf,
    upbuf,
    khi,
    klo,
    chi,
    clo,
    dpart,
    dsib,
    drecv,
    dsum,
    zbuf,
    s1_send,
    s1_recv,
    ag_send,
    ag_recv,
    sib_send,
    sib_recv,
    down_send,
    down_recv,
    up_send,
    up_recv,
    ds_send,
    ds_recv,
    dr_send,
    dr_recv,
    dz_send,
    dz_recv,
    dw_send,
    dw_recv,
    da_send,
    da_recv,
    db_send,
    db_recv,
):
    R, C, L, B, S, W = sizes
    F = R // C
    lane_parts = W // LANES
    RC = R // lane_parts
    r = lax.axis_index("prow")
    c = lax.axis_index("pcol")
    panels, pats, cols, dias = (p0, p1), (pat0, pat1), (col0, col1), (dia0, dia1)
    total = R * C
    me = r * C + c
    sibling = r + 1 - 2 * lax.rem(r, 2)

    barrier = pltpu.get_barrier_semaphore()

    @pl.loop(1, total)
    def _(i):
        other = lax.rem(me + i, total)
        pl.semaphore_signal(
            barrier, inc=1, device_id=(lax.div(other, C), lax.rem(other, C)), device_id_type=MESH
        )

    pl.semaphore_wait(barrier, total - 1)

    def row_part(k):
        return lax.div(k, lane_parts)

    def lanes(k):
        return pl.ds(pl.multiple_of(lax.rem(k, lane_parts) * LANES, LANES), LANES)

    def remote(src, dst, send, recv, row, column):
        return pltpu.make_async_remote_copy(
            src_ref=src,
            dst_ref=dst,
            send_sem=send,
            recv_sem=recv,
            device_id=(row, column),
            device_id_type=MESH,
        )

    plane = lax.rem(r, C)
    source = lax.div(r, C) * C + c
    own_plane = plane == c

    def first_copy(n, d):
        k = lax.rem(r + d, R)
        src = panels[n].at[:, row_part(k), :, lanes(k)]
        dst = xbuf.at[n, :, source, row_part(k), :, lanes(k)]
        return remote(src, dst, s1_send.at[n, d], s1_recv.at[n, source], k, plane)

    def first_local(n):
        src = panels[n].at[:, row_part(r), :, lanes(r)]
        dst = xbuf.at[n, :, source, row_part(r), :, lanes(r)]
        return pltpu.make_async_copy(src, dst, s1_recv.at[n, source])

    def first_wait(n, q):
        part = xbuf.at[n, :, q, row_part(r), :, lanes(r)]
        pltpu.make_async_copy(part, part, s1_recv.at[n, q]).wait()

    def strip(n, k):
        return xbuf.at[n, :, :, row_part(k), :, lanes(k)]

    def gather_copy(n, j):
        part = strip(n, r)
        return remote(
            part, part, ag_send.at[n, j], ag_recv.at[n, j], lax.rem(r + 2 * j, R), c
        )

    def gather_wait(n, j):
        part = strip(n, lax.rem(r + R - 2 * j, R))
        pltpu.make_async_copy(part, part, ag_recv.at[n, j]).wait()

    def sibling_copy(n, j):
        part = strip(n, lax.rem(r + R - 2 * j, R))
        return remote(part, part, sib_send.at[n, j], sib_recv.at[n, j], sibling, c)

    def sibling_wait(n, j):
        part = strip(n, lax.rem(sibling + R - 2 * j, R))
        pltpu.make_async_copy(part, part, sib_recv.at[n, j]).wait()

    def sum_piece(n, z):
        return ybuf.at[n, :, pl.ds(pl.multiple_of(z * S, S), S), :]

    def down_copy(n, z):
        row = lax.rem(c + C - 1, C)
        return remote(
            sum_piece(n, z), downbuf.at[n, z], down_send.at[n, z], down_recv.at[n, z], r, row
        )

    def up_copy(n, z):
        row = lax.rem(c + 1, C)
        return remote(sum_piece(n, z), upbuf.at[n, z], up_send.at[n, z], up_recv.at[n, z], r, row)

    def local_wait(part, sem):
        pltpu.make_async_copy(part, part, sem).wait()

    def add_piece(n, z, buf, sem):
        local_wait(buf.at[n, z], sem.at[n, z])
        rows = pl.ds(pl.multiple_of(z * S, S), S)
        for l in range(L):
            ybuf[n, l, rows, :] = ybuf[n, l, rows, :] + buf[n, z, l]

    def pass_sums(n, i):
        @pl.when(c > i)
        def _():
            @pl.when(c < C - 1)
            def _():
                add_piece(n, i, downbuf, down_recv)

            down_copy(n, i).start()

        top = C - 1 - i

        @pl.when(c < top)
        def _():
            @pl.when(c > 0)
            def _():
                add_piece(n, top, upbuf, up_recv)

            up_copy(n, top).start()

    def own_sums(n):
        @pl.when(c < C - 1)
        def _():
            add_piece(n, c, downbuf, down_recv)

        @pl.when(c > 0)
        def _():
            add_piece(n, c, upbuf, up_recv)

    def chain_wait_send(n):
        for i in range(C - 1):

            @pl.when(c > i)
            def _():
                down_copy(n, i).wait_send()

            @pl.when(c < C - 1 - i)
            def _():
                up_copy(n, C - 1 - i).wait_send()

    def ring(j):
        return lax.rem(r + 2 * j, R)

    def diag_sib_copy(n, j):
        k = lax.rem(sibling + 2 * j, R)
        return remote(
            dpart.at[n, k], dsib.at[n, j], ds_send.at[n, j], ds_recv.at[n, j], sibling, c
        )

    def diag_row_copy(n, j):
        return remote(
            dpart.at[n, ring(j)], drecv.at[n, j], dr_send.at[n, j], dr_recv.at[n, j], ring(j), c
        )

    def diag_piece(ref, z):
        groups = C // lane_parts if C > lane_parts else 1
        height = W // R // groups
        row = pl.multiple_of(lax.div(z, C // groups) * height, height)
        width = W // (C // groups)
        lane = pl.multiple_of(lax.rem(z, C // groups) * width, width)
        return ref.at[pl.ds(row, height), pl.ds(lane, width)]

    def diag_col_copy(n, d):
        z = lax.rem(c + d, C)
        return remote(
            diag_piece(dsum.at[n], z), zbuf.at[n, d], dz_send.at[n, d], dz_recv.at[n, d], r, z
        )

    def diag_whole_copy(n, d):
        part = diag_piece(dias[n].at[r], c)
        return remote(part, part, dw_send.at[n, d], dw_recv.at[n, d], r, lax.rem(c + d, C))

    def diag_all_copy(n, j):
        part = dias[n].at[r]
        return remote(part, part, da_send.at[n, j], da_recv.at[n, j], ring(j), c)

    def diag_last_copy(n, j):
        part = dias[n].at[lax.rem(r + R - 2 * j, R)]
        return remote(part, part, db_send.at[n, j], db_recv.at[n, j], sibling, c)

    def start_first(n):
        for d in range(1, R):
            first_copy(n, d).start()

        @pl.when(own_plane)
        def _():
            first_local(n).start()

        @pl.when(jnp.logical_not(own_plane))
        def _():
            first_copy(n, 0).start()

    def start_gather(n):
        for q in range(F * C):
            first_wait(n, q)
        for j in range(1, R // 2):
            gather_copy(n, j).start()
        sibling_copy(n, 0).start()

    def forward(n):
        for j in range(1, R // 2):
            gather_wait(n, j)
            sibling_copy(n, j).start()

    def multiply(n):
        for j in range(R // 2):
            sibling_wait(n, j)

        @pl.loop(0, L * F * C)
        def _(i):
            l = lax.div(i, F * C)
            q = lax.rem(i, F * C)
            kept = pats[n][l * R + lax.div(q, C) * C + c].astype(F32)
            rows = pl.ds(pl.multiple_of(i * S, S), S)
            high, low = halves(xbuf[n, l, q].reshape(S, W) * kept)
            xhi[rows, :] = high
            xlo[rows, :] = low

        @pl.loop(0, L)
        def _(l):
            rows = pl.ds(pl.multiple_of(l * B, B), B)
            ybuf[n, l] = dot3(
                (ahi[rows, :], alo[rows, :]), (xhi[...], xlo[...]), ((1,), (0,))
            )


    def finish_column(n):
        own_sums(n)
        for l in range(L):
            kept = pats[n][l * R + r].astype(F32)
            value = ybuf[n, l, pl.ds(pl.multiple_of(c * S, S), S), :]
            value = -(value * kept)
            cols[n][l] = value
            rows = slice(l * S, (l + 1) * S)
            chi[rows, :], clo[rows, :] = halves(value)
            khi[rows, :], klo[rows, :] = halves(panels[n][l].reshape(S, W) * kept)
        part = dot3((khi[...], klo[...]), (chi[...], clo[...]), ((0,), (0,)))
        dpart[n] = part.reshape(R, W // R, W)
        for j in range(R // 2):
            diag_sib_copy(n, j).start()

    def diag_rows(n):
        for j in range(R // 2):
            diag_sib_copy(n, j).wait_recv()
            dpart[n, ring(j)] = dpart[n, ring(j)] + dsib[n, j]
            if j > 0:
                diag_row_copy(n, j).start()

    def diag_cols(n):
        value = dpart[n, r]
        for j in range(1, R // 2):
            diag_row_copy(n, j).wait_recv()
            value = value + drecv[n, j]
        dsum[n] = value
        for d in range(1, C):
            diag_col_copy(n, d).start()

    def diag_whole(n):
        value = diag_piece(dsum.at[n], c)[...]
        for d in range(1, C):
            diag_col_copy(n, d).wait_recv()
            value = value + zbuf[n, d]
        diag_piece(dias[n].at[r], c)[...] = value
        for d in range(1, C):
            diag_whole_copy(n, d).start()

    def diag_all(n):
        for d in range(1, C):
            part = diag_piece(dias[n].at[r], lax.rem(c + C - d, C))
            local_wait(part, dw_recv.at[n, d])
        for j in range(1, R // 2):
            diag_all_copy(n, j).start()
        diag_last_copy(n, 0).start()

    def diag_last(n):
        for j in range(1, R // 2):
            local_wait(dias[n].at[lax.rem(r + R - 2 * j, R)], da_recv.at[n, j])
            diag_last_copy(n, j).start()

    start_first(0)
    start_first(1)

    tile = min(B, 64)
    parts = ahi.shape[1] // LANES

    @pl.loop(0, L * B // tile)
    def _(i):
        rows = pl.ds(pl.multiple_of(i * tile, tile), tile)
        for h in range(parts):
            value = mat[pl.ds(i * tile * parts + h, tile, stride=parts), :]
            across = slice(h * LANES, (h + 1) * LANES)
            ahi[rows, across], alo[rows, across] = halves(value)

    start_gather(0)
    forward(0)
    start_gather(1)
    multiply(0)
    pass_sums(0, 0)
    forward(1)
    for i in range(1, C - 1):
        pass_sums(0, i)
    multiply(1)
    pass_sums(1, 0)
    finish_column(0)
    diag_rows(0)
    for i in range(1, C - 1):
        pass_sums(1, i)
    diag_cols(0)
    finish_column(1)
    diag_whole(0)
    diag_rows(1)
    diag_all(0)
    diag_cols(1)
    diag_last(0)
    diag_whole(1)
    diag_all(1)
    diag_last(1)
    for n in range(2):
        for j in range(R // 2):
            local_wait(dias[n].at[lax.rem(sibling + R - 2 * j, R)], db_recv.at[n, j])
        for d in range(1, R):
            first_copy(n, d).wait_send()

        @pl.when(jnp.logical_not(own_plane))
        def _():
            first_copy(n, 0).wait_send()

        for j in range(R // 2):
            if j > 0:
                gather_copy(n, j).wait_send()
                diag_row_copy(n, j).wait_send()
                diag_all_copy(n, j).wait_send()
            sibling_copy(n, j).wait_send()
            diag_sib_copy(n, j).wait_send()
            diag_last_copy(n, j).wait_send()
        chain_wait_send(n)
        for d in range(1, C):
            diag_col_copy(n, d).wait_send()
            diag_whole_copy(n, d).wait_send()


def body(R, C, inverse, first, second, diag_first, diag_second, pat_first, pat_second):
    L, _, B, M, _, _ = inverse.shape
    S, W = first.shape[2:]
    F = R // C
    RC = R // (W // LANES)
    matrix = inverse.reshape(L * B * M * B // LANES, LANES)
    panels = [p.reshape(L, RC, S // RC, W) for p in (first, second)]
    vmem = pl.BlockSpec(memory_space=pltpu.VMEM)
    smem = pl.BlockSpec(memory_space=pltpu.SMEM)
    dma = pltpu.SemaphoreType.DMA
    part = W // R
    groups = max(1, C * LANES // W)
    flops = 3 * 2 * L * B * M * B * 2 * W
    col0, col1, sum0, sum1 = pl.pallas_call(
        functools.partial(kernel, (R, C, L, B, S, W)),
        out_shape=[jax.ShapeDtypeStruct((L, S, W), F32)] * 2
        + [jax.ShapeDtypeStruct((R, part, W), F32)] * 2,
        in_specs=[vmem] * 3 + [smem] * 2,
        out_specs=[vmem] * 4,
        scratch_shapes=[
            pltpu.VMEM((2, L, F * C, RC, S // RC, W), F32),
            pltpu.VMEM((L * B, M * B), BF16),
            pltpu.VMEM((L * B, M * B), BF16),
            pltpu.VMEM((M * B, W), BF16),
            pltpu.VMEM((M * B, W), BF16),
            pltpu.VMEM((2, L, B, W), F32),
            pltpu.VMEM((2, C, L, S, W), F32),
            pltpu.VMEM((2, C, L, S, W), F32),
            pltpu.VMEM((L * S, W), BF16),
            pltpu.VMEM((L * S, W), BF16),
            pltpu.VMEM((L * S, W), BF16),
            pltpu.VMEM((L * S, W), BF16),
            pltpu.VMEM((2, R, part, W), F32),
            pltpu.VMEM((2, R // 2, part, W), F32),
            pltpu.VMEM((2, R // 2, part, W), F32),
            pltpu.VMEM((2, part, W), F32),
            pltpu.VMEM((2, C, part // groups, W * groups // C), F32),
            dma((2, R)),
            dma((2, F * C)),
            dma((2, R // 2)),
            dma((2, R // 2)),
            dma((2, R // 2)),
            dma((2, R // 2)),
            dma((2, C)),
            dma((2, C)),
            dma((2, C)),
            dma((2, C)),
            dma((2, R // 2)),
            dma((2, R // 2)),
            dma((2, R // 2)),
            dma((2, R // 2)),
            dma((2, C)),
            dma((2, C)),
            dma((2, C)),
            dma((2, C)),
            dma((2, R // 2)),
            dma((2, R // 2)),
            dma((2, R // 2)),
            dma((2, R // 2)),
        ],
        compiler_params=pltpu.CompilerParams(
            collective_id=0, has_side_effects=True, vmem_limit_bytes=56 * 1024 * 1024
        ),
        cost_estimate=pl.CostEstimate(
            flops=flops, bytes_accessed=4 * L * B * M * B, transcendentals=0
        ),
    )(matrix, *panels, pat_first, pat_second)
    return (
        col0[:, None],
        col1[:, None],
        diag_first - sum0.reshape(W, W),
        diag_second - sum1.reshape(W, W),
    )


def solution(mesh):
    placed = (
        P(None, "prow", None, None, "pcol", None),
        P(None, "prow", "pcol", None),
        P(None, "prow", "pcol", None),
        P(),
        P(),
        P(),
        P(),
    )
    return jax.shard_map(
        functools.partial(body, mesh.shape["prow"], mesh.shape["pcol"]),
        mesh=mesh,
        in_specs=placed,
        out_specs=(P(None, "prow", "pcol", None), P(None, "prow", "pcol", None), P(), P()),
        check_vma=False,
    )
```

```python
import functools

import jax
import jax.numpy as jnp
from jax import lax
from jax.experimental import pallas as pl
from jax.experimental.pallas import tpu as pltpu
from jax.sharding import PartitionSpec as P

MESH = pl.DeviceIdType.MESH
LANES = 128
F32 = jnp.float32
BF16 = jnp.bfloat16


def halves(value):
    high = value.astype(BF16)
    return high, (value - high.astype(F32)).astype(BF16)


def dot3(left, right, dims):
    def one(a, b):
        return lax.dot_general(a, b, (dims, ((), ())), preferred_element_type=F32)

    return one(left[0], right[0]) + (one(left[0], right[1]) + one(left[1], right[0]))


def kernel(
    sizes,
    mat,
    p0,
    p1,
    pat0,
    pat1,
    col0,
    col1,
    dia0,
    dia1,
    xbuf,
    ahi,
    alo,
    xhi,
    xlo,
    ybuf,
    rsbuf,
    khi,
    klo,
    chi,
    clo,
    dpart,
    dsib,
    drecv,
    dsum,
    zbuf,
    s1_send,
    s1_recv,
    ag_send,
    ag_recv,
    sib_send,
    sib_recv,
    rs_send,
    rs_recv,
    ds_send,
    ds_recv,
    dr_send,
    dr_recv,
    dz_send,
    dz_recv,
    dw_send,
    dw_recv,
    da_send,
    da_recv,
    db_send,
    db_recv,
):
    R, C, L, B, S, W = sizes
    F = R // C
    lane_parts = W // LANES
    RC = R // lane_parts
    r = lax.axis_index("prow")
    c = lax.axis_index("pcol")
    panels, pats, cols, dias = (p0, p1), (pat0, pat1), (col0, col1), (dia0, dia1)
    total = R * C
    me = r * C + c
    sibling = r + 1 - 2 * lax.rem(r, 2)

    barrier = pltpu.get_barrier_semaphore()

    @pl.loop(1, total)
    def _(i):
        other = lax.rem(me + i, total)
        pl.semaphore_signal(
            barrier, inc=1, device_id=(lax.div(other, C), lax.rem(other, C)), device_id_type=MESH
        )

    pl.semaphore_wait(barrier, total - 1)

    def row_part(k):
        return lax.div(k, lane_parts)

    def lanes(k):
        return pl.ds(pl.multiple_of(lax.rem(k, lane_parts) * LANES, LANES), LANES)

    def remote(src, dst, send, recv, row, column):
        return pltpu.make_async_remote_copy(
            src_ref=src,
            dst_ref=dst,
            send_sem=send,
            recv_sem=recv,
            device_id=(row, column),
            device_id_type=MESH,
        )

    plane = lax.rem(r, C)
    source = lax.div(r, C) * C + c
    own_plane = plane == c

    def first_copy(n, d):
        k = lax.rem(r + d, R)
        src = panels[n].at[:, row_part(k), :, lanes(k)]
        dst = xbuf.at[n, k, :, source]
        return remote(src, dst, s1_send.at[n, d], s1_recv.at[n, source], k, plane)

    def first_local(n):
        src = panels[n].at[:, row_part(r), :, lanes(r)]
        dst = xbuf.at[n, r, :, source]
        return pltpu.make_async_copy(src, dst, s1_recv.at[n, source])

    def first_wait(n, q):
        part = xbuf.at[n, r, :, q]
        pltpu.make_async_copy(part, part, s1_recv.at[n, q]).wait()

    def strip(n, k):
        return xbuf.at[n, k]

    def gather_copy(n, j):
        part = strip(n, r)
        return remote(
            part, part, ag_send.at[n, j], ag_recv.at[n, j], lax.rem(r + 2 * j, R), c
        )

    def gather_wait(n, j):
        part = strip(n, lax.rem(r + R - 2 * j, R))
        pltpu.make_async_copy(part, part, ag_recv.at[n, j]).wait()

    def sibling_copy(n, j):
        part = strip(n, lax.rem(r + R - 2 * j, R))
        return remote(part, part, sib_send.at[n, j], sib_recv.at[n, j], sibling, c)

    def sibling_wait(n, j):
        part = strip(n, lax.rem(sibling + R - 2 * j, R))
        pltpu.make_async_copy(part, part, sib_recv.at[n, j]).wait()

    def scatter_copy(n, d):
        z = lax.rem(c + d, C)
        return remote(
            ybuf.at[n, :, pl.ds(pl.multiple_of(z * S, S), S), :],
            rsbuf.at[n, d],
            rs_send.at[n, d],
            rs_recv.at[n, d],
            r,
            z,
        )

    def local_wait(part, sem):
        pltpu.make_async_copy(part, part, sem).wait()

    def ring(j):
        return lax.rem(r + 2 * j, R)

    def diag_sib_copy(n, j):
        k = lax.rem(sibling + 2 * j, R)
        return remote(
            dpart.at[n, k], dsib.at[n, j], ds_send.at[n, j], ds_recv.at[n, j], sibling, c
        )

    def diag_row_copy(n, j):
        return remote(
            dpart.at[n, ring(j)], drecv.at[n, j], dr_send.at[n, j], dr_recv.at[n, j], ring(j), c
        )

    def diag_piece(ref, z):
        groups = C // lane_parts if C > lane_parts else 1
        height = W // R // groups
        row = pl.multiple_of(lax.div(z, C // groups) * height, height)
        width = W // (C // groups)
        lane = pl.multiple_of(lax.rem(z, C // groups) * width, width)
        return ref.at[pl.ds(row, height), pl.ds(lane, width)]

    def diag_col_copy(n, d):
        z = lax.rem(c + d, C)
        return remote(
            diag_piece(dsum.at[n], z), zbuf.at[n, d], dz_send.at[n, d], dz_recv.at[n, d], r, z
        )

    def diag_whole_copy(n, d):
        part = diag_piece(dias[n].at[r], c)
        return remote(part, part, dw_send.at[n, d], dw_recv.at[n, d], r, lax.rem(c + d, C))

    def diag_all_copy(n, j):
        part = dias[n].at[r]
        return remote(part, part, da_send.at[n, j], da_recv.at[n, j], ring(j), c)

    def diag_last_copy(n, j):
        part = dias[n].at[lax.rem(r + R - 2 * j, R)]
        return remote(part, part, db_send.at[n, j], db_recv.at[n, j], sibling, c)

    def start_first(n):
        for d in range(1, R):
            first_copy(n, d).start()

        @pl.when(own_plane)
        def _():
            first_local(n).start()

        @pl.when(jnp.logical_not(own_plane))
        def _():
            first_copy(n, 0).start()

    def start_gather(n):
        for q in range(F * C):
            first_wait(n, q)
        for j in range(1, R // 2):
            gather_copy(n, j).start()
        sibling_copy(n, 0).start()

    def forward(n):
        for j in range(1, R // 2):
            gather_wait(n, j)
            sibling_copy(n, j).start()

    def multiply(n):
        for j in range(R // 2):
            sibling_wait(n, j)

        @pl.loop(0, L * F * C)
        def _(i):
            l = lax.div(i, F * C)
            q = lax.rem(i, F * C)
            kept = pats[n][l * R + lax.div(q, C) * C + c].astype(F32)
            bands = [
                jnp.concatenate(
                    [xbuf[n, g * lane_parts + h, l, q] for h in range(lane_parts)], axis=1
                )
                for g in range(RC)
            ]
            rows = pl.ds(pl.multiple_of(i * S, S), S)
            xhi[rows, :], xlo[rows, :] = halves(jnp.concatenate(bands, axis=0) * kept)

        @pl.loop(0, L)
        def _(l):
            rows = pl.ds(pl.multiple_of(l * B, B), B)
            ybuf[n, l] = dot3(
                (ahi[rows, :], alo[rows, :]), (xhi[...], xlo[...]), ((1,), (0,))
            )


    def scatter(n):
        for d in range(1, C):
            scatter_copy(n, d).start()

    def finish_column(n):
        for d in range(1, C):
            scatter_copy(n, d).wait_recv()
        for l in range(L):
            kept = pats[n][l * R + r].astype(F32)
            value = ybuf[n, l, pl.ds(pl.multiple_of(c * S, S), S), :]
            for d in range(1, C):
                value = value + rsbuf[n, d, l]
            value = -(value * kept)
            cols[n][l] = value
            rows = slice(l * S, (l + 1) * S)
            chi[rows, :], clo[rows, :] = halves(value)
            khi[rows, :], klo[rows, :] = halves(panels[n][l].reshape(S, W) * kept)
        part = dot3((khi[...], klo[...]), (chi[...], clo[...]), ((0,), (0,)))
        dpart[n] = part.reshape(R, W // R, W)
        for j in range(R // 2):
            diag_sib_copy(n, j).start()

    def diag_rows(n):
        for j in range(R // 2):
            diag_sib_copy(n, j).wait_recv()
            dpart[n, ring(j)] = dpart[n, ring(j)] + dsib[n, j]
            if j > 0:
                diag_row_copy(n, j).start()

    def diag_cols(n):
        value = dpart[n, r]
        for j in range(1, R // 2):
            diag_row_copy(n, j).wait_recv()
            value = value + drecv[n, j]
        dsum[n] = value
        for d in range(1, C):
            diag_col_copy(n, d).start()

    def diag_whole(n):
        value = diag_piece(dsum.at[n], c)[...]
        for d in range(1, C):
            diag_col_copy(n, d).wait_recv()
            value = value + zbuf[n, d]
        diag_piece(dias[n].at[r], c)[...] = value
        for d in range(1, C):
            diag_whole_copy(n, d).start()

    def diag_all(n):
        for d in range(1, C):
            part = diag_piece(dias[n].at[r], lax.rem(c + C - d, C))
            local_wait(part, dw_recv.at[n, d])
        for j in range(1, R // 2):
            diag_all_copy(n, j).start()
        diag_last_copy(n, 0).start()

    def diag_last(n):
        for j in range(1, R // 2):
            local_wait(dias[n].at[lax.rem(r + R - 2 * j, R)], da_recv.at[n, j])
            diag_last_copy(n, j).start()

    start_first(0)
    start_gather(0)
    start_first(1)

    tile = min(B, 64)
    parts = ahi.shape[1] // LANES

    @pl.loop(0, L * B // tile)
    def _(i):
        rows = pl.ds(pl.multiple_of(i * tile, tile), tile)
        for h in range(parts):
            value = mat[pl.ds(i * tile * parts + h, tile, stride=parts), :]
            across = slice(h * LANES, (h + 1) * LANES)
            ahi[rows, across], alo[rows, across] = halves(value)

    forward(0)
    start_gather(1)
    multiply(0)
    scatter(0)
    forward(1)
    multiply(1)
    scatter(1)
    finish_column(0)
    diag_rows(0)
    diag_cols(0)
    diag_whole(0)
    finish_column(1)
    diag_all(0)
    diag_rows(1)
    diag_last(0)
    diag_cols(1)
    diag_whole(1)
    diag_all(1)
    diag_last(1)
    for n in range(2):
        for j in range(R // 2):
            local_wait(dias[n].at[lax.rem(sibling + R - 2 * j, R)], db_recv.at[n, j])
        for d in range(1, R):
            first_copy(n, d).wait_send()

        @pl.when(jnp.logical_not(own_plane))
        def _():
            first_copy(n, 0).wait_send()

        for j in range(R // 2):
            if j > 0:
                gather_copy(n, j).wait_send()
                diag_row_copy(n, j).wait_send()
                diag_all_copy(n, j).wait_send()
            sibling_copy(n, j).wait_send()
            diag_sib_copy(n, j).wait_send()
            diag_last_copy(n, j).wait_send()
        for d in range(1, C):
            scatter_copy(n, d).wait_send()
            diag_col_copy(n, d).wait_send()
            diag_whole_copy(n, d).wait_send()


def body(R, C, inverse, first, second, diag_first, diag_second, pat_first, pat_second):
    L, _, B, M, _, _ = inverse.shape
    S, W = first.shape[2:]
    F = R // C
    RC = R // (W // LANES)
    matrix = inverse.reshape(L * B * M * B // LANES, LANES)
    panels = [p.reshape(L, RC, S // RC, W) for p in (first, second)]
    vmem = pl.BlockSpec(memory_space=pltpu.VMEM)
    smem = pl.BlockSpec(memory_space=pltpu.SMEM)
    dma = pltpu.SemaphoreType.DMA
    part = W // R
    groups = max(1, C * LANES // W)
    flops = 3 * 2 * L * B * M * B * 2 * W
    col0, col1, sum0, sum1 = pl.pallas_call(
        functools.partial(kernel, (R, C, L, B, S, W)),
        out_shape=[jax.ShapeDtypeStruct((L, S, W), F32)] * 2
        + [jax.ShapeDtypeStruct((R, part, W), F32)] * 2,
        in_specs=[vmem] * 3 + [smem] * 2,
        out_specs=[vmem] * 4,
        scratch_shapes=[
            pltpu.VMEM((2, R, L, F * C, S // RC, LANES), F32),
            pltpu.VMEM((L * B, M * B), BF16),
            pltpu.VMEM((L * B, M * B), BF16),
            pltpu.VMEM((M * B, W), BF16),
            pltpu.VMEM((M * B, W), BF16),
            pltpu.VMEM((2, L, B, W), F32),
            pltpu.VMEM((2, C, L, S, W), F32),
            pltpu.VMEM((L * S, W), BF16),
            pltpu.VMEM((L * S, W), BF16),
            pltpu.VMEM((L * S, W), BF16),
            pltpu.VMEM((L * S, W), BF16),
            pltpu.VMEM((2, R, part, W), F32),
            pltpu.VMEM((2, R // 2, part, W), F32),
            pltpu.VMEM((2, R // 2, part, W), F32),
            pltpu.VMEM((2, part, W), F32),
            pltpu.VMEM((2, C, part // groups, W * groups // C), F32),
            dma((2, R)),
            dma((2, F * C)),
            dma((2, R // 2)),
            dma((2, R // 2)),
            dma((2, R // 2)),
            dma((2, R // 2)),
            dma((2, C)),
            dma((2, C)),
            dma((2, R // 2)),
            dma((2, R // 2)),
            dma((2, R // 2)),
            dma((2, R // 2)),
            dma((2, C)),
            dma((2, C)),
            dma((2, C)),
            dma((2, C)),
            dma((2, R // 2)),
            dma((2, R // 2)),
            dma((2, R // 2)),
            dma((2, R // 2)),
        ],
        compiler_params=pltpu.CompilerParams(
            collective_id=0, has_side_effects=True, vmem_limit_bytes=56 * 1024 * 1024
        ),
        cost_estimate=pl.CostEstimate(
            flops=flops, bytes_accessed=4 * L * B * M * B, transcendentals=0
        ),
    )(matrix, *panels, pat_first, pat_second)
    return (
        col0[:, None],
        col1[:, None],
        diag_first - sum0.reshape(W, W),
        diag_second - sum1.reshape(W, W),
    )


def solution(mesh):
    placed = (
        P(None, "prow", None, None, "pcol", None),
        P(None, "prow", "pcol", None),
        P(None, "prow", "pcol", None),
        P(),
        P(),
        P(),
        P(),
    )
    return jax.shard_map(
        functools.partial(body, mesh.shape["prow"], mesh.shape["pcol"]),
        mesh=mesh,
        in_specs=placed,
        out_specs=(P(None, "prow", "pcol", None), P(None, "prow", "pcol", None), P(), P()),
        check_vma=False,
    )
```
